256 devices in a mesh: rank: 4 (over x_lo, core), basis: 64 (over y, x_hi, z).
Axes of the slice: x: 4 (x_hi: 2, x_lo: 2; x = x_hi * 2 + x_lo), y: 4, z: 8, core: 2. Of those that a mesh axis runs over, the one named last changes fastest.
Arguments:
- factors: bfloat16 [4, 16384, 1024], P('rank', 'basis'), may hold values from -0.796875 to 0.796875
Outputs:
- exchange_matrix: float32 [16384, 16384], P('basis', 'rank')
The draws below stay inside these ranges and needn't reach their ends.
All inputs are finite; a program needn't handle non-finite values.
Results may differ from the reference program's by a relative error of at most 0.012.
Values may be sent and summed in bfloat16 or wider, within the bound.
A program may use at most 128 MiB of HBM per device.

```python
import jax
import jax.numpy as jnp
from jax import lax

NBF = 16384
NOCC = 1024
QDEV = 1
NQ = 4
N_RANK = 4


def shard_levels(own_key, shape, shards, smallest, high):
    loudness = 1.0
    for axis_at, parts in shards:
        draws = jax.random.uniform(jax.random.fold_in(jax.random.fold_in(own_key, 6), axis_at), (parts,), jnp.float32, smallest / len(shards), high / len(shards))
        loudness = loudness * jnp.repeat(jnp.exp(draws), shape[axis_at] // parts).reshape((-1,) + (1,) * (len(shape) - 1 - axis_at))
    return loudness


def scatter_about(own_key, shape, deviation, bound, split=(), kind=jnp.bfloat16):
    entries = jax.random.normal(own_key, shape, jnp.float32) * deviation
    if len(split) > 0:
        entries = shard_levels(own_key, shape, split, -0.22, 0.18) * entries
    return jnp.clip(entries, min=-bound, max=bound).astype(kind)


def setup_inputs(seed: int = 0) -> dict:
    arg_keys = jax.random.split(jax.random.key(seed), 2)
    factors = scatter_about(arg_keys[0], (NQ, NBF, NOCC), 0.1, 0.796875, ((0, 4), (1, 64)))
    return {"factors": factors}


def reference(factors):
    total = jnp.zeros((NBF, NBF), jnp.float32)
    for block in range(N_RANK):
        piece = factors[block * QDEV:(block + 1) * QDEV].astype(jnp.float32)
        flat = jnp.transpose(piece, (1, 0, 2)).reshape(NBF, QDEV * NOCC)
        part = jnp.dot(flat, flat.T, precision=lax.Precision.HIGHEST)
        rounded = lax.optimization_barrier(part.astype(jnp.bfloat16))
        total = total + rounded.astype(jnp.float32)
    return total
```

```python
import functools

import jax
import jax.numpy as jnp
from jax import lax
from jax.experimental import pallas as pl
from jax.experimental.pallas import tpu as pltpu
from jax.sharding import PartitionSpec as P

MESH = pl.DeviceIdType.MESH
NY, NX, NZ = 4, 2, 8
ND = 5
F32, BF16 = jnp.float32, jnp.bfloat16


def kernel(
    src, out, rows_p, rows_q, dsend, drecv, acc, xsend, xrecv, direct, flipped,
    own_sem, p_ssem, p_rsem, q_ssem, q_rsem, d_ssem, d_rsem, x_ssem, x_rsem,
    a_ssem, a_rsem, b_ssem, b_rsem, l_sem,
):
    rank = lax.axis_index("rank")
    basis = lax.axis_index("basis")
    lo, core = rank // 2, rank % 2
    z = basis % NZ
    xh = (basis // NZ) % NX
    y = basis // (NZ * NX)

    def at(y_, x_, z_):
        return (y_ * NX + x_) * NZ + z_

    other_core = (lo * 2 + (1 - core), basis)
    other_lo = ((1 - lo) * 2 + core, basis)
    other_x = (rank, at(y, 1 - xh, z))
    y_up = (rank, at((y + 1) % NY, xh, z))
    y_down = (rank, at((y + 3) % NY, xh, z))
    z_down = (rank, at(y, xh, (z + NZ - 1) % NZ))

    def z_off(d):
        return (rank, at(y, xh, (z + d) % NZ))

    def columns(x_, z_):
        width = src.shape[0]
        start = pl.multiple_of((x_ * NZ + z_) * width, width)
        return out.at[:, pl.ds(start, width)]

    def mirror(x_):
        return (y, at(rank, x_, z))

    barrier = pltpu.get_barrier_semaphore()
    partners = [other_core, other_lo, other_x, y_up, y_down]
    partners += [z_off(d) for d in (1, 2, 3, 5, 6, 7)]
    for who in partners:
        pl.semaphore_signal(barrier, inc=1, device_id=who, device_id_type=MESH)

    @pl.when(rank != y)
    def _():
        for x_ in range(NX):
            pl.semaphore_signal(
                barrier, inc=1, device_id=mirror(x_), device_id_type=MESH
            )

    pl.semaphore_wait(barrier, len(partners) + jnp.where(rank != y, NX, 0))

    def remote(a, b, ssem, rsem, who):
        return pltpu.make_async_remote_copy(
            src_ref=a, dst_ref=b, send_sem=ssem, recv_sem=rsem,
            device_id=who, device_id_type=MESH,
        )

    def p_copy(d):
        a = src if d == 0 else rows_p.at[d]
        return remote(a, rows_p.at[d + 1], p_ssem.at[d], p_rsem.at[d + 1], z_down)

    def q_slot(dy, flip):
        return ((y + dy) % NY) * NX + (xh + flip) % NX

    def q_copy(i, dy, flip, who):
        slot = q_slot(dy, flip)
        a = src if (dy, flip) == (0, 0) else rows_q.at[slot]
        return remote(a, rows_q.at[slot], q_ssem.at[i], q_rsem.at[slot], who)

    def q_wait(dy, flip):
        slot = q_slot(dy, flip)
        remote(
            src, rows_q.at[slot], q_ssem.at[0], q_rsem.at[slot], other_x
        ).wait_recv()

    def p_wait(d):
        remote(src, rows_p.at[d], p_ssem.at[0], p_rsem.at[d], z_down).wait_recv()

    p_sends = [p_copy(d) for d in range(ND - 1)]
    q_sends = [
        q_copy(0, 0, 0, y_up),
        q_copy(1, 0, 0, y_down),
        q_copy(2, 0, 0, other_x),
        q_copy(3, 0, 1, y_up),
        q_copy(4, 0, 1, y_down),
        q_copy(5, 1, 0, y_down),
        q_copy(6, 3, 1, y_up),
    ]
    p_sends[0].start()
    q_sends[0].start()
    q_sends[1].start()
    q_sends[2].start()
    own_p = pltpu.make_async_copy(src, rows_p.at[0], own_sem.at[0])
    own_q = pltpu.make_async_copy(src, rows_q.at[q_slot(0, 0)], own_sem.at[1])
    own_p.start()
    own_q.start()
    own_p.wait()
    own_q.wait()

    def unit(g, h):
        m = ((g + 1) // 2) % 2
        dy = (g + 1) // 2 + 2 * m * h
        flip = m * (g // 2) + (1 - m) * h
        return (y + dy) % NY, (xh + flip) % NX

    def each(g0, g1, d0, d1, body):
        nd = d1 - d0

        def step(k, carry):
            d = d0 + k % nd
            rest = k // nd
            yc, xc = unit(g0 + rest // 2, rest % 2)
            body(d, yc, xc)
            return carry

        lax.fori_loop(0, (g1 - g0) * 2 * nd, step, 0)

    def d_copy(d, yc, xc):
        s = ((yc // 2) * NX + xc) * ND + d
        return remote(dsend.at[s], drecv.at[s], d_ssem.at[s], d_rsem.at[s], other_core)

    def x_copy(d, xc):
        s = xc * ND + d
        return remote(xsend.at[s], xrecv.at[s], x_ssem.at[s], x_rsem.at[s], other_lo)

    def a_copy(d, xc):
        s = xc * ND + d
        return remote(
            direct.at[s], columns(xc, z), a_ssem.at[s], a_rsem.at[s], z_off(d)
        )

    def b_copy(d, xc):
        s, r = xc * ND + d, xh * ND + d
        return remote(
            flipped.at[s], columns(xh, (z + d) % NZ), b_ssem.at[s], b_rsem.at[r],
            mirror(xc),
        )

    def b_local(d, xc):
        s, r = xc * ND + d, xh * ND + d
        return pltpu.make_async_copy(
            flipped.at[s], columns(xh, (z + d) % NZ), b_rsem.at[r]
        )

    def a_local(xc):
        return pltpu.make_async_copy(
            direct.at[xc * ND], columns(xc, z), l_sem.at[xc]
        )

    def to_self(xc):
        return jnp.logical_and(rank == y, xc == xh)

    def multiply(d, yc, xc):
        s = ((yc // 2) * NX + xc) * ND + d
        t = lax.dot_general(
            rows_p[d], rows_q[yc * NX + xc], (((1,), (1,)), ((), ())),
            preferred_element_type=F32,
        )

        @pl.when(yc % 2 != core)
        def _():
            dsend[s] = t.astype(BF16)
            d_copy(d, yc, xc).start()

        @pl.when(yc % 2 == core)
        def _():
            acc[s] = t

    def pass_on(d, yc, xc):
        s = ((yc // 2) * NX + xc) * ND + d

        @pl.when(jnp.logical_and(yc % 2 == core, yc // 2 != lo))
        def _():
            d_copy(d, yc, xc).wait_recv()
            xsend[xc * ND + d] = (acc[s] + drecv[s].astype(F32)).astype(BF16)
            x_copy(d, xc).start()

    def finish(d, yc, xc):
        s = ((yc // 2) * NX + xc) * ND + d
        e = xc * ND + d

        @pl.when(yc == rank)
        def _():
            d_copy(d, yc, xc).wait_recv()
            x_copy(d, xc).wait_recv()
            v = acc[s] + drecv[s].astype(F32) + xrecv[e].astype(F32)

            @pl.when(d < ND - 1)
            def _():
                direct[e] = v.astype(BF16)

            @pl.when(d == 0)
            def _():
                a_local(xc).start()

            @pl.when(jnp.logical_and(d > 0, d < ND - 1))
            def _():
                a_copy(d, xc).start()

            @pl.when(d > 0)
            def _():
                flipped[e] = v.T.astype(BF16)

                @pl.when(to_self(xc))
                def _():
                    b_local(d, xc).start()

                @pl.when(jnp.logical_not(to_self(xc)))
                def _():
                    b_copy(d, xc).start()

    def run(*boxes):
        for body in (multiply, pass_on, finish):
            for g0, g1, d0, d1 in boxes:
                each(g0, g1, d0, d1, body)

    p_wait(1)
    p_sends[1].start()
    q_wait(0, 1)
    q_sends[3].start()
    q_sends[4].start()
    q_wait(1, 0)
    q_sends[5].start()
    q_wait(3, 0)
    run((0, 2, 0, 2))
    p_wait(2)
    p_sends[2].start()
    q_wait(3, 1)
    q_sends[6].start()
    q_wait(1, 1)
    run((0, 2, 2, 3), (2, 3, 0, 3))
    p_wait(3)
    p_sends[3].start()
    q_wait(2, 0)
    q_wait(2, 1)
    run((0, 3, 3, 4), (3, 4, 0, 4))
    p_wait(4)
    run((0, 4, 4, 5))

    for c in p_sends + q_sends:
        c.wait_send()

    def drain(d, yc, xc):
        @pl.when(yc % 2 != core)
        def _():
            d_copy(d, yc, xc).wait_send()

        @pl.when(jnp.logical_and(yc % 2 == core, yc // 2 != lo))
        def _():
            x_copy(d, xc).wait_send()

        @pl.when(yc == rank)
        def _():
            @pl.when(d == 0)
            def _():
                a_local(xc).wait()

            @pl.when(jnp.logical_and(d > 0, d < ND - 1))
            def _():
                a_copy(d, xc).wait()

            @pl.when(d > 0)
            def _():

                @pl.when(jnp.logical_not(to_self(xc)))
                def _():
                    b_copy(d, xc).wait_send()

    each(0, 4, 0, ND, drain)

    def landed(k, carry):
        d, xs = 1 + k % (ND - 1), k // (ND - 1)
        pltpu.make_async_copy(
            flipped.at[xs * ND + d], columns(xs, (z + d) % NZ), b_rsem.at[xs * ND + d]
        ).wait()
        return carry

    lax.fori_loop(0, NX * (ND - 1), landed, 0)


def solution(mesh):
    def local(factors):
        _, rows, depth = factors.shape
        tile = (rows, rows)
        n = NX * ND
        dma = pltpu.SemaphoreType.DMA
        blocks = pl.pallas_call(
            kernel,
            out_shape=jax.ShapeDtypeStruct((rows, NX * NZ * rows), BF16),
            in_specs=[pl.BlockSpec(memory_space=pl.ANY)],
            out_specs=pl.BlockSpec(memory_space=pl.ANY),
            scratch_shapes=[
                pltpu.VMEM((ND, rows, depth), BF16),
                pltpu.VMEM((NY * NX, rows, depth), BF16),
                pltpu.VMEM((2 * n, *tile), BF16),
                pltpu.VMEM((2 * n, *tile), BF16),
                pltpu.VMEM((2 * n, *tile), F32),
                pltpu.VMEM((n, *tile), BF16),
                pltpu.VMEM((n, *tile), BF16),
                pltpu.VMEM((n, *tile), BF16),
                pltpu.VMEM((n, *tile), BF16),
                dma((2,)),
                dma((ND,)), dma((ND,)),
                dma((7,)), dma((NY * NX,)),
                dma((2 * n,)), dma((2 * n,)),
                dma((n,)), dma((n,)),
                dma((n,)), dma((n,)),
                dma((n,)), dma((n,)),
                dma((NX,)),
            ],
            compiler_params=pltpu.CompilerParams(
                collective_id=0, has_side_effects=True, vmem_limit_bytes=40 * 2**20
            ),
        )(factors[0])
        return blocks.astype(F32)

    return jax.shard_map(
        local,
        mesh=mesh,
        in_specs=(P("rank", "basis", None),),
        out_specs=P("basis", "rank"),
        check_vma=False,
    )
```

```python
import functools

import jax
import jax.numpy as jnp
from jax import lax
from jax.experimental import pallas as pl
from jax.experimental.pallas import tpu as pltpu
from jax.sharding import PartitionSpec as P

MESH = pl.DeviceIdType.MESH
NY, NX, NZ = 4, 2, 8
F32, BF16 = jnp.float32, jnp.bfloat16

NQ, ND = NY * NX, 5

def both(*pairs):
    return tuple((q, d) for p, d in pairs for q in (p, p + 1))


FIRST = both((0, 1), (0, 0)) + ((2, 1), (6, 1))
SECOND = both((6, 2), (0, 2), (6, 0)) + ((4, 2), (4, 1), (7, 1), (2, 2))
THIRD = both((0, 3), (2, 3), (4, 3), (6, 3))
LATE = ((3, 2), (5, 2), (3, 1), (5, 1))
KEPT = both((2, 0), (4, 0))
LAST = both((0, 4), (2, 4), (4, 4), (6, 4))
STEPS = (FIRST, SECOND, THIRD, LATE, KEPT, LAST)


def kernel(
    src, out, rows, dsend, drecv, acc, xsend, xrecv, direct, flipped,
    own_sem, p_ssem, p_rsem, q_ssem, q_rsem, d_ssem, d_rsem, x_ssem, x_rsem,
    a_ssem, a_rsem, b_ssem, b_rsem,
):
    rank = lax.axis_index("rank")
    basis = lax.axis_index("basis")
    lo, core = rank // 2, rank % 2
    z = basis % NZ
    xh = (basis // NZ) % NX
    y = basis // (NZ * NX)

    def at(y_, x_, z_):
        return (y_ * NX + x_) * NZ + z_

    other_core = (lo * 2 + (1 - core), basis)
    other_lo = ((1 - lo) * 2 + core, basis)
    other_x = (rank, at(y, 1 - xh, z))
    beside = ((1 - lo) * 2 + core, at(y, 1 - xh, z))
    y_up = (rank, at((y + 1) % NY, xh, z))
    y_down = (rank, at((y + 3) % NY, xh, z))

    def z_off(d):
        return (rank, at(y, xh, (z + d) % NZ))

    z_up, z_down = z_off(1), z_off(NZ - 1)

    half = src.shape[0] // 2

    def columns(x_, z_):
        width = src.shape[0]
        start = pl.multiple_of((x_ * NZ + z_) * width, width)
        return out.at[:, pl.ds(start, width)]

    def mirror(x_):
        return (y, at(rank, x_, z))

    barrier = pltpu.get_barrier_semaphore()
    partners = [other_core, other_lo, other_x, beside, y_up, y_down]
    partners += [z_off(d) for d in (1, 2, 3, 5, 6, 7)]
    for who in partners:
        pl.semaphore_signal(barrier, inc=1, device_id=who, device_id_type=MESH)

    @pl.when(rank != y)
    def _():
        for x_ in range(NX):
            pl.semaphore_signal(
                barrier, inc=1, device_id=mirror(x_), device_id_type=MESH
            )

    pl.semaphore_wait(barrier, len(partners) + jnp.where(rank != y, NX, 0))

    def remote(a, b, ssem, rsem, who):
        return pltpu.make_async_remote_copy(
            src_ref=a, dst_ref=b, send_sem=ssem, recv_sem=rsem,
            device_id=who, device_id_type=MESH,
        )

    def p_block(d):
        return src if d == 0 else rows.at[NQ + d - 1]

    def p_down(d):
        a, b = p_block(d), p_block(d + 1)
        if d == 3:
            a, b = a.at[pl.ds(0, half)], b.at[pl.ds(0, half)]
        return remote(a, b, p_ssem.at[d], p_rsem.at[d], z_down)

    def p_up(d):
        a, b = p_block((NZ - d) % NZ), p_block(NZ - d - 1)
        if d == 3:
            a, b = a.at[pl.ds(half, half)], b.at[pl.ds(half, half)]
        return remote(a, b, p_ssem.at[4 + d], p_rsem.at[4 + d], z_up)

    def q_slot(dy, flip):
        return ((y + dy) % NY) * NX + (xh + flip) % NX

    def q_copy(i, dy, flip, who):
        slot = q_slot(dy, flip)
        a = src if (dy, flip) == (0, 0) else rows.at[slot]
        return remote(a, rows.at[slot], q_ssem.at[i], q_rsem.at[slot], who)

    def q_wait(dy, flip):
        slot = q_slot(dy, flip)
        remote(
            src, rows.at[slot], q_ssem.at[0], q_rsem.at[slot], other_x
        ).wait_recv()

    down = [p_down(d) for d in range(4)]
    up = [p_up(d) for d in range(4)]
    q_sends = [
        q_copy(0, 0, 0, y_down),
        q_copy(1, 0, 0, y_up),
        q_copy(2, 0, 0, other_x),
        q_copy(3, 1, 0, y_down),
        q_copy(4, 0, 1, y_up),
        q_copy(5, 0, 1, y_down),
        q_copy(6, 3, 1, y_up),
    ]
    down[0].start()
    up[0].start()
    q_sends[0].start()
    q_sends[1].start()
    q_sends[2].start()
    own = pltpu.make_async_copy(src, rows.at[q_slot(0, 0)], own_sem.at[0])
    own.start()
    own.wait()

    def each(units, body):
        for first in range(0, len(units), 10):
            part = units[first : first + 10]
            qs = sum(q * 8**k for k, (q, _) in enumerate(part))
            ds = sum(d * 8**k for k, (_, d) in enumerate(part))

            def step(k, carry):
                qs, ds = carry
                body(qs % 8, ds % 8)
                return qs // 8, ds // 8

            lax.fori_loop(0, len(part), step, (jnp.int32(qs), jnp.int32(ds)))

    def block(q):
        return (y + q // 2) % NY, (xh + q % 2) % NX

    def full(yc, xc, d):
        return ((yc // 2) * NX + xc) * ND + d

    def d_copy(s):
        return remote(dsend.at[s], drecv.at[s], d_ssem.at[s], d_rsem.at[s], other_core)

    def x_copy(d, xc):
        e = xc * ND + d
        to = ((1 - lo) * 2 + core, at(y, jnp.where(d == 0, 1 - xh, xh), z))
        return remote(xsend.at[e], xrecv.at[e], x_ssem.at[e], x_rsem.at[e], to)

    def away(yc, d):
        return jnp.where((yc + y) % 2 == 0, d, (NZ - d) % NZ)

    def a_copy(d, xc):
        e = xc * ND + d
        return remote(
            direct.at[e], columns(xc, z), a_ssem.at[e], a_rsem.at[e],
            z_off(away(rank, d)),
        )

    def a_local(xc):
        e = xc * ND
        return pltpu.make_async_copy(direct.at[e], columns(xc, z), a_rsem.at[e])

    def b_place(d, x_):
        return columns(x_, (z + away(rank, d)) % NZ)

    def b_copy(d, xc):
        e, r = xc * ND + d, xh * ND + d
        return remote(
            flipped.at[e], b_place(d, xh), b_ssem.at[e], b_rsem.at[r], mirror(xc)
        )

    def b_local(d, x_):
        e = x_ * ND + d
        return pltpu.make_async_copy(flipped.at[e], b_place(d, x_), b_rsem.at[e])

    def goes_direct(q, d):
        return d < ND - 1

    def goes_flipped(q, d):
        return d > 0

    def left(yc, d):
        side = jnp.where(yc // 2 == lo, xh, 1 - xh)
        return rows[jnp.where(d == 0, y * NX + side, NQ + away(yc, d) - 1)]

    def place(t, yc, xc, d):
        s = full(yc, xc, d)

        @pl.when(yc % 2 != core)
        def _():
            dsend[s] = t.astype(BF16)
            d_copy(s).start()

        @pl.when(yc % 2 == core)
        def _():
            acc[s] = t

    def product(a, b):
        return lax.dot_general(
            a, b, (((1,), (1,)), ((), ())), preferred_element_type=F32
        )

    def multiply(q, d):
        yc, xc = block(q)
        place(product(left(yc, d), rows[yc * NX + xc]), yc, xc, d)

    def multiply_both(yc, d):
        n, depth = src.shape
        b = rows[pl.ds(yc * NX, NX)].reshape(NX * n, depth)
        t = product(left(yc, d), b)
        for xc in range(NX):
            place(t[:, xc * n : (xc + 1) * n], yc, xc, d)

    def pairs(todo):
        each(todo, lambda q, d: multiply_both((y + q // 2) % NY, d))

    def all_pairs(d):
        def step(k, carry):
            multiply_both(((k // 2 + 1 + lo) % 2) * 2 + k % 2, d)
            return carry

        lax.fori_loop(0, NY, step, 0)

    def pass_on(q, d):
        yc, xc = block(q)
        s, e = full(yc, xc, d), xc * ND + d

        @pl.when(jnp.logical_and(yc % 2 == core, yc // 2 != lo))
        def _():
            d_copy(s).wait_recv()
            xsend[e] = (acc[s] + drecv[s].astype(F32)).astype(BF16)
            x_copy(d, xc).start()

    def finish(q, d):
        yc, xc = block(q)
        s, e = full(yc, xc, d), xc * ND + d

        @pl.when(yc == rank)
        def _():
            d_copy(s).wait_recv()
            x_copy(d, xc).wait_recv()
            v = acc[s] + drecv[s].astype(F32) + xrecv[e].astype(F32)

            @pl.when(goes_direct(q, d))
            def _():
                direct[e] = v.astype(BF16)

                @pl.when(d == 0)
                def _():
                    a_local(xc).start()

                @pl.when(d > 0)
                def _():
                    a_copy(d, xc).start()

            @pl.when(goes_flipped(q, d))
            def _():
                flipped[e] = v.T.astype(BF16)

                @pl.when(q == 0)
                def _():
                    b_local(d, xh).start()

                @pl.when(q > 0)
                def _():
                    b_copy(d, xc).start()

    down[0].wait_recv()
    down[1].start()
    up[0].wait_recv()
    up[1].start()
    q_wait(0, 1)
    q_sends[4].start()
    q_wait(1, 0)
    q_sends[3].start()
    q_sends[5].start()
    pairs(((0, 1), (0, 0)))
    q_wait(3, 0)
    each(((2, 1), (6, 1)), multiply)
    each(FIRST, pass_on)
    each(FIRST, finish)

    down[1].wait_recv()
    down[2].start()
    up[1].wait_recv()
    up[2].start()
    q_wait(3, 1)
    q_sends[6].start()
    pairs(((6, 2), (0, 2)))
    q_wait(2, 0)
    each(((4, 2), (4, 1), (7, 1), (2, 2)), multiply)
    each(SECOND[:4], pass_on)
    pairs(((6, 0),))
    each(SECOND[4:], pass_on)

    down[2].wait_recv()
    down[3].start()
    up[2].wait_recv()
    up[3].start()
    each(SECOND, finish)
    q_wait(1, 1)
    q_wait(2, 1)
    all_pairs(3)
    each(THIRD, pass_on)
    each(LATE, multiply)
    each(LATE, pass_on)
    pairs(((2, 0), (4, 0)))
    each(KEPT, pass_on)
    each(THIRD, finish)

    down[3].wait_recv()
    up[3].wait_recv()
    all_pairs(4)
    each(LAST, pass_on)
    for units in (LATE, LAST, KEPT):
        each(units, finish)

    for c in down + up + q_sends:
        c.wait_send()

    def drain(q, d):
        yc, xc = block(q)

        @pl.when(yc % 2 != core)
        def _():
            d_copy(full(yc, xc, d)).wait_send()

        @pl.when(jnp.logical_and(yc % 2 == core, yc // 2 != lo))
        def _():
            x_copy(d, xc).wait_send()

        @pl.when(yc == rank)
        def _():
            @pl.when(goes_direct(q, d))
            def _():
                @pl.when(d == 0)
                def _():
                    a_local(xc).wait()

                @pl.when(d > 0)
                def _():
                    a_copy(d, xc).wait()

            @pl.when(jnp.logical_and(q > 0, goes_flipped(q, d)))
            def _():
                b_copy(d, xc).wait_send()

        @pl.when(jnp.logical_and((rank + q // 2) % NY == y, goes_flipped(q, d)))
        def _():
            b_local(d, (xh + q) % NX).wait()

    for units in STEPS:
        each(units, drain)


def solution(mesh):
    def local(factors):
        _, rows, depth = factors.shape
        tile = (rows, rows)
        n = NX * ND
        dma = pltpu.SemaphoreType.DMA
        blocks = pl.pallas_call(
            kernel,
            out_shape=jax.ShapeDtypeStruct((rows, NX * NZ * rows), BF16),
            in_specs=[pl.BlockSpec(memory_space=pl.ANY)],
            out_specs=pl.BlockSpec(memory_space=pl.ANY),
            scratch_shapes=[
                pltpu.VMEM((NQ + NZ - 1, rows, depth), BF16),
                pltpu.VMEM((2 * n, *tile), BF16),
                pltpu.VMEM((2 * n, *tile), BF16),
                pltpu.VMEM((2 * n, *tile), F32),
                pltpu.VMEM((n, *tile), BF16),
                pltpu.VMEM((n, *tile), BF16),
                pltpu.VMEM((n, *tile), BF16),
                pltpu.VMEM((n, *tile), BF16),
                dma((1,)),
                dma((NZ,)), dma((NZ,)),
                dma((7,)), dma((NQ,)),
                dma((2 * n,)), dma((2 * n,)),
                dma((n,)), dma((n,)),
                dma((n,)), dma((n,)),
                dma((n,)), dma((n,)),
            ],
            compiler_params=pltpu.CompilerParams(
                collective_id=0, has_side_effects=True, vmem_limit_bytes=44 * 2**20
            ),
        )(factors[0])
        return blocks.astype(F32)

    return jax.shard_map(
        local,
        mesh=mesh,
        in_specs=(P("rank", "basis", None),),
        out_specs=P("basis", "rank"),
        check_vma=False,
    )
```

```python
import functools

import jax
import jax.numpy as jnp
from jax import lax
from jax.experimental import pallas as pl
from jax.experimental.pallas import tpu as pltpu
from jax.sharding import PartitionSpec as P

MESH = pl.DeviceIdType.MESH
NY, NX, NZ = 4, 2, 8
F32, BF16 = jnp.float32, jnp.bfloat16

NQ, ND = NY * NX, 5

def both(*pairs):
    return tuple((q, d) for p, d in pairs for q in (p, p + 1))


FIRST = both((0, 1), (0, 0)) + ((2, 1), (6, 1))
SECOND = both((2, 2), (6, 2), (0, 2)) + ((3, 1), (7, 1), (4, 2), (4, 1)) + both((6, 0))
LATE = ((5, 2), (5, 1))
THIRD = both((0, 3), (2, 3), (4, 3), (6, 3))
KEPT = both((2, 0), (4, 0))
LAST = both((0, 4), (2, 4), (4, 4), (6, 4))
STEPS = (FIRST, SECOND, LATE, THIRD, KEPT, LAST)


def kernel(
    src, out, rows, dsend, drecv, acc, xsend, xrecv, direct, flipped,
    own_sem, p_ssem, p_rsem, q_ssem, q_rsem, d_ssem, d_rsem, x_ssem, x_rsem,
    a_ssem, a_rsem, b_ssem, b_rsem,
):
    rank = lax.axis_index("rank")
    basis = lax.axis_index("basis")
    lo, core = rank // 2, rank % 2
    z = basis % NZ
    xh = (basis // NZ) % NX
    y = basis // (NZ * NX)

    def at(y_, x_, z_):
        return (y_ * NX + x_) * NZ + z_

    other_core = (lo * 2 + (1 - core), basis)
    other_lo = ((1 - lo) * 2 + core, basis)
    other_x = (rank, at(y, 1 - xh, z))
    beside = ((1 - lo) * 2 + core, at(y, 1 - xh, z))
    y_up = (rank, at((y + 1) % NY, xh, z))
    y_down = (rank, at((y + 3) % NY, xh, z))

    def z_off(d):
        return (rank, at(y, xh, (z + d) % NZ))

    z_up, z_down = z_off(1), z_off(NZ - 1)

    half = src.shape[0] // 2

    def columns(x_, z_):
        width = src.shape[0]
        start = pl.multiple_of((x_ * NZ + z_) * width, width)
        return out.at[:, pl.ds(start, width)]

    def mirror(x_):
        return (y, at(rank, x_, z))

    barrier = pltpu.get_barrier_semaphore()
    partners = [other_core, other_lo, other_x, beside, y_up, y_down]
    partners += [z_off(d) for d in (1, 2, 3, 5, 6, 7)]
    for who in partners:
        pl.semaphore_signal(barrier, inc=1, device_id=who, device_id_type=MESH)

    @pl.when(rank != y)
    def _():
        for x_ in range(NX):
            pl.semaphore_signal(
                barrier, inc=1, device_id=mirror(x_), device_id_type=MESH
            )

    pl.semaphore_wait(barrier, len(partners) + jnp.where(rank != y, NX, 0))

    def remote(a, b, ssem, rsem, who):
        return pltpu.make_async_remote_copy(
            src_ref=a, dst_ref=b, send_sem=ssem, recv_sem=rsem,
            device_id=who, device_id_type=MESH,
        )

    def p_block(d):
        return src if d == 0 else rows.at[NQ + d - 1]

    def p_down(d):
        a, b = p_block(d), p_block(d + 1)
        if d == 3:
            a, b = a.at[pl.ds(0, half)], b.at[pl.ds(0, half)]
        return remote(a, b, p_ssem.at[d], p_rsem.at[d], z_down)

    def p_up(d):
        a, b = p_block((NZ - d) % NZ), p_block(NZ - d - 1)
        if d == 3:
            a, b = a.at[pl.ds(half, half)], b.at[pl.ds(half, half)]
        return remote(a, b, p_ssem.at[4 + d], p_rsem.at[4 + d], z_up)

    def q_slot(dy, flip):
        return ((y + dy) % NY) * NX + (xh + flip) % NX

    def q_copy(i, dy, flip, who, part=None):
        at_slot = rows.at[q_slot(dy, flip)]
        a = src if (dy, flip) == (0, 0) else at_slot
        sem = q_slot(dy, flip)
        if part is not None:
            a, at_slot = (r.at[pl.ds(part * half, half)] for r in (a, at_slot))
            sem = NQ + part
        return remote(a, at_slot, q_ssem.at[i], q_rsem.at[sem], who)

    def q_wait(dy, flip):
        slot = q_slot(dy, flip)
        remote(
            src, rows.at[slot], q_ssem.at[0], q_rsem.at[slot], other_x
        ).wait_recv()

    def q_wait_part(dy, flip, part):
        place = rows.at[q_slot(dy, flip), pl.ds(part * half, half)]
        remote(
            src.at[pl.ds(0, half)], place, q_ssem.at[0], q_rsem.at[NQ + part], other_x
        ).wait_recv()

    down = [p_down(d) for d in range(4)]
    up = [p_up(d) for d in range(4)]
    q_sends = [
        q_copy(0, 0, 0, y_down),
        q_copy(1, 0, 0, y_up),
        q_copy(2, 0, 0, other_x),
        q_copy(3, 1, 0, y_down),
        q_copy(4, 1, 0, other_x),
        q_copy(5, 0, 1, y_up),
        q_copy(6, 1, 1, y_down, 0),
        q_copy(7, 3, 1, y_up, 1),
    ]
    down[0].start()
    up[0].start()
    q_sends[0].start()
    q_sends[1].start()
    q_sends[2].start()
    own = pltpu.make_async_copy(src, rows.at[q_slot(0, 0)], own_sem.at[0])
    own.start()
    own.wait()

    def each(units, body):
        for first in range(0, len(units), 10):
            part = units[first : first + 10]
            qs = sum(q * 8**k for k, (q, _) in enumerate(part))
            ds = sum(d * 8**k for k, (_, d) in enumerate(part))

            def step(k, carry):
                qs, ds = carry
                body(qs % 8, ds % 8)
                return qs // 8, ds // 8

            lax.fori_loop(0, len(part), step, (jnp.int32(qs), jnp.int32(ds)))

    def block(q):
        return (y + q // 2) % NY, (xh + q % 2) % NX

    def full(yc, xc, d):
        return ((yc // 2) * NX + xc) * ND + d

    def d_copy(s):
        return remote(dsend.at[s], drecv.at[s], d_ssem.at[s], d_rsem.at[s], other_core)

    def x_copy(d, xc):
        e = xc * ND + d
        to = ((1 - lo) * 2 + core, at(y, jnp.where(d == 0, 1 - xh, xh), z))
        return remote(xsend.at[e], xrecv.at[e], x_ssem.at[e], x_rsem.at[e], to)

    def away(yc, d):
        return jnp.where((yc + y) % 2 == 0, d, (NZ - d) % NZ)

    def a_copy(d, xc):
        e = xc * ND + d
        return remote(
            direct.at[e], columns(xc, z), a_ssem.at[e], a_rsem.at[e],
            z_off(away(rank, d)),
        )

    def a_local(xc):
        e = xc * ND
        return pltpu.make_async_copy(direct.at[e], columns(xc, z), a_rsem.at[e])

    def b_place(d, x_):
        return columns(x_, (z + away(rank, d)) % NZ)

    def b_copy(d, xc):
        e, r = xc * ND + d, xh * ND + d
        return remote(
            flipped.at[e], b_place(d, xh), b_ssem.at[e], b_rsem.at[r], mirror(xc)
        )

    def b_local(d, x_):
        e = x_ * ND + d
        return pltpu.make_async_copy(flipped.at[e], b_place(d, x_), b_rsem.at[e])

    def goes_direct(q, d):
        return d < ND - 1

    def goes_flipped(q, d):
        return d > 0

    def left(yc, d):
        side = jnp.where(yc // 2 == lo, xh, 1 - xh)
        return rows[jnp.where(d == 0, y * NX + side, NQ + away(yc, d) - 1)]

    def place(t, yc, xc, d):
        s = full(yc, xc, d)

        @pl.when(yc % 2 != core)
        def _():
            dsend[s] = t.astype(BF16)
            d_copy(s).start()

        @pl.when(yc % 2 == core)
        def _():
            acc[s] = t

    def product(a, b):
        return lax.dot_general(
            a, b, (((1,), (1,)), ((), ())), preferred_element_type=F32
        )

    def multiply(q, d):
        yc, xc = block(q)
        place(product(left(yc, d), rows[yc * NX + xc]), yc, xc, d)

    def multiply_both(yc, d):
        n, depth = src.shape
        b = rows[pl.ds(yc * NX, NX)].reshape(NX * n, depth)
        t = product(left(yc, d), b)
        for xc in range(NX):
            place(t[:, xc * n : (xc + 1) * n], yc, xc, d)

    def pairs(todo):
        each(todo, lambda q, d: multiply_both((y + q // 2) % NY, d))

    def all_pairs(d):
        def step(k, carry):
            multiply_both(((k // 2 + 1 + lo) % 2) * 2 + k % 2, d)
            return carry

        lax.fori_loop(0, NY, step, 0)

    def pass_on(q, d):
        yc, xc = block(q)
        s, e = full(yc, xc, d), xc * ND + d

        @pl.when(jnp.logical_and(yc % 2 == core, yc // 2 != lo))
        def _():
            d_copy(s).wait_recv()
            xsend[e] = (acc[s] + drecv[s].astype(F32)).astype(BF16)
            x_copy(d, xc).start()

    def finish(q, d):
        yc, xc = block(q)
        s, e = full(yc, xc, d), xc * ND + d

        @pl.when(yc == rank)
        def _():
            d_copy(s).wait_recv()
            x_copy(d, xc).wait_recv()
            v = acc[s] + drecv[s].astype(F32) + xrecv[e].astype(F32)

            @pl.when(goes_direct(q, d))
            def _():
                direct[e] = v.astype(BF16)

                @pl.when(d == 0)
                def _():
                    a_local(xc).start()

                @pl.when(d > 0)
                def _():
                    a_copy(d, xc).start()

            @pl.when(goes_flipped(q, d))
            def _():
                flipped[e] = v.T.astype(BF16)

                @pl.when(q == 0)
                def _():
                    b_local(d, xh).start()

                @pl.when(q > 0)
                def _():
                    b_copy(d, xc).start()

    down[0].wait_recv()
    down[1].start()
    up[0].wait_recv()
    up[1].start()
    q_wait(0, 1)
    q_sends[5].start()
    q_wait(1, 0)
    q_sends[3].start()
    q_sends[4].start()
    pairs(((0, 1), (0, 0)))
    q_wait(3, 0)
    each(((2, 1), (6, 1)), multiply)
    each(FIRST, pass_on)

    down[1].wait_recv()
    down[2].start()
    up[1].wait_recv()
    up[2].start()
    q_wait(3, 1)
    q_sends[7].start()
    q_wait(1, 1)
    q_sends[6].start()
    pairs(((2, 2), (6, 2), (0, 2)))
    each(SECOND[:6], pass_on)
    q_wait(2, 0)
    each(SECOND[6:10], multiply)
    each(SECOND[6:10], pass_on)
    pairs(((6, 0),))
    each(SECOND[10:], pass_on)
    each(FIRST, finish)
    q_wait_part(2, 1, 0)
    q_wait_part(2, 1, 1)
    each(LATE, multiply)
    each(LATE, pass_on)

    down[2].wait_recv()
    down[3].start()
    up[2].wait_recv()
    up[3].start()
    all_pairs(3)
    each(THIRD, pass_on)
    each(SECOND, finish)
    each(LATE, finish)
    pairs(((2, 0), (4, 0)))
    each(KEPT, pass_on)
    each(THIRD, finish)

    down[3].wait_recv()
    up[3].wait_recv()
    all_pairs(4)
    each(LAST, pass_on)
    each(KEPT, finish)
    each(LAST, finish)

    for c in down + up + q_sends:
        c.wait_send()

    def drain(q, d):
        yc, xc = block(q)

        @pl.when(yc % 2 != core)
        def _():
            d_copy(full(yc, xc, d)).wait_send()

        @pl.when(jnp.logical_and(yc % 2 == core, yc // 2 != lo))
        def _():
            x_copy(d, xc).wait_send()

        @pl.when(yc == rank)
        def _():
            @pl.when(goes_direct(q, d))
            def _():
                @pl.when(d == 0)
                def _():
                    a_local(xc).wait()

                @pl.when(d > 0)
                def _():
                    a_copy(d, xc).wait()

            @pl.when(jnp.logical_and(q > 0, goes_flipped(q, d)))
            def _():
                b_copy(d, xc).wait_send()

        @pl.when(jnp.logical_and((rank + q // 2) % NY == y, goes_flipped(q, d)))
        def _():
            b_local(d, (xh + q) % NX).wait()

    for units in STEPS:
        each(units, drain)


def solution(mesh):
    def local(factors):
        _, rows, depth = factors.shape
        tile = (rows, rows)
        n = NX * ND
        dma = pltpu.SemaphoreType.DMA
        blocks = pl.pallas_call(
            kernel,
            out_shape=jax.ShapeDtypeStruct((rows, NX * NZ * rows), BF16),
            in_specs=[pl.BlockSpec(memory_space=pltpu.HBM)],
            out_specs=pl.BlockSpec(memory_space=pl.ANY),
            scratch_shapes=[
                pltpu.VMEM((NQ + NZ - 1, rows, depth), BF16),
                pltpu.VMEM((2 * n, *tile), BF16),
                pltpu.VMEM((2 * n, *tile), BF16),
                pltpu.VMEM((2 * n, *tile), F32),
                pltpu.VMEM((n, *tile), BF16),
                pltpu.VMEM((n, *tile), BF16),
                pltpu.VMEM((n, *tile), BF16),
                pltpu.VMEM((n, *tile), BF16),
                dma((1,)),
                dma((NZ,)), dma((NZ,)),
                dma((8,)), dma((NQ + 2,)),
                dma((2 * n,)), dma((2 * n,)),
                dma((n,)), dma((n,)),
                dma((n,)), dma((n,)),
                dma((n,)), dma((n,)),
            ],
            compiler_params=pltpu.CompilerParams(
                collective_id=0, has_side_effects=True, vmem_limit_bytes=44 * 2**20
            ),
        )(factors[0])
        return blocks.astype(F32)

    return jax.shard_map(
        local,
        mesh=mesh,
        in_specs=(P("rank", "basis", None),),
        out_specs=P("basis", "rank"),
        check_vma=False,
    )
```

```python
import functools

import jax
import jax.numpy as jnp
from jax import lax
from jax.experimental import pallas as pl
from jax.experimental.pallas import tpu as pltpu
from jax.sharding import PartitionSpec as P

MESH = pl.DeviceIdType.MESH
NY, NX, NZ = 4, 2, 8
F32, BF16 = jnp.float32, jnp.bfloat16

NQ, ND = NY * NX, 5

def both(*pairs):
    return tuple((q, d) for p, d in pairs for q in (p, p + 1))


FIRST = both((0, 1), (0, 0)) + ((2, 1), (6, 1))
SECOND = both((2, 2), (6, 2), (0, 2)) + ((3, 1), (7, 1), (4, 2), (4, 1)) + both((6, 0))
LATE = ((5, 2), (5, 1))
THIRD = both((0, 3), (2, 3), (4, 3), (6, 3))
KEPT = both((2, 0), (4, 0))
LAST = both((0, 4), (2, 4), (4, 4), (6, 4))
STEPS = (FIRST, SECOND, LATE, THIRD, KEPT, LAST)


def kernel(
    src, out, rows, dsend, drecv, acc, xsend, xrecv, direct, flipped,
    own_sem, p_ssem, p_rsem, q_ssem, q_rsem, d_ssem, d_rsem, x_ssem, x_rsem,
    a_ssem, a_rsem, b_ssem, b_rsem,
):
    rank = lax.axis_index("rank")
    basis = lax.axis_index("basis")
    lo, core = rank // 2, rank % 2
    z = basis % NZ
    xh = (basis // NZ) % NX
    y = basis // (NZ * NX)

    def at(y_, x_, z_):
        return (y_ * NX + x_) * NZ + z_

    other_core = (lo * 2 + (1 - core), basis)
    other_lo = ((1 - lo) * 2 + core, basis)
    other_x = (rank, at(y, 1 - xh, z))
    beside = ((1 - lo) * 2 + core, at(y, 1 - xh, z))
    y_up = (rank, at((y + 1) % NY, xh, z))
    y_down = (rank, at((y + 3) % NY, xh, z))

    def z_off(d):
        return (rank, at(y, xh, (z + d) % NZ))

    z_up, z_down = z_off(1), z_off(NZ - 1)

    half = src.shape[0] // 2

    def columns(x_, z_):
        width = src.shape[0]
        start = pl.multiple_of((x_ * NZ + z_) * width, width)
        return out.at[:, pl.ds(start, width)]

    def mirror(x_):
        return (y, at(rank, x_, z))

    barrier = pltpu.get_barrier_semaphore()
    partners = [other_core, other_lo, other_x, beside, y_up, y_down]
    partners += [z_off(d) for d in range(1, NZ)]
    for who in partners:
        pl.semaphore_signal(barrier, inc=1, device_id=who, device_id_type=MESH)

    @pl.when(rank != y)
    def _():
        for x_ in range(NX):
            pl.semaphore_signal(
                barrier, inc=1, device_id=mirror(x_), device_id_type=MESH
            )

    pl.semaphore_wait(barrier, len(partners) + jnp.where(rank != y, NX, 0))

    def remote(a, b, ssem, rsem, who):
        return pltpu.make_async_remote_copy(
            src_ref=a, dst_ref=b, send_sem=ssem, recv_sem=rsem,
            device_id=who, device_id_type=MESH,
        )

    def p_block(d):
        return src if d == 0 else rows.at[NQ + d - 1]

    def p_down(d):
        a, b = p_block(d), p_block(d + 1)
        if d == 3:
            a, b = a.at[pl.ds(0, half)], b.at[pl.ds(0, half)]
        return remote(a, b, p_ssem.at[d], p_rsem.at[d], z_down)

    def p_up(d):
        a, b = p_block((NZ - d) % NZ), p_block(NZ - d - 1)
        if d == 3:
            a, b = a.at[pl.ds(half, half)], b.at[pl.ds(half, half)]
        return remote(a, b, p_ssem.at[4 + d], p_rsem.at[4 + d], z_up)

    def q_slot(dy, flip):
        return ((y + dy) % NY) * NX + (xh + flip) % NX

    def q_copy(i, dy, flip, who, part=None):
        at_slot = rows.at[q_slot(dy, flip)]
        a = src if (dy, flip) == (0, 0) else at_slot
        sem = q_slot(dy, flip)
        if part is not None:
            a, at_slot = (r.at[pl.ds(part * half, half)] for r in (a, at_slot))
            sem = NQ + part
        return remote(a, at_slot, q_ssem.at[i], q_rsem.at[sem], who)

    def q_wait(dy, flip):
        slot = q_slot(dy, flip)
        remote(
            src, rows.at[slot], q_ssem.at[0], q_rsem.at[slot], other_x
        ).wait_recv()

    def q_wait_part(dy, flip, part):
        place = rows.at[q_slot(dy, flip), pl.ds(part * half, half)]
        remote(
            src.at[pl.ds(0, half)], place, q_ssem.at[0], q_rsem.at[NQ + part], other_x
        ).wait_recv()

    down = [p_down(d) for d in range(4)]
    up = [p_up(d) for d in range(4)]
    q_sends = [
        q_copy(0, 0, 0, y_down),
        q_copy(1, 0, 0, y_up),
        q_copy(2, 0, 0, other_x),
        q_copy(3, 1, 0, y_down),
        q_copy(4, 1, 0, other_x),
        q_copy(5, 0, 1, y_up),
        q_copy(6, 1, 1, y_down, 0),
        q_copy(7, 3, 1, y_up, 1),
    ]
    down[0].start()
    up[0].start()
    q_sends[0].start()
    q_sends[1].start()
    q_sends[2].start()
    own = pltpu.make_async_copy(src, rows.at[q_slot(0, 0)], own_sem.at[0])
    own.start()
    own.wait()

    def each(units, body):
        for first in range(0, len(units), 10):
            part = units[first : first + 10]
            qs = sum(q * 8**k for k, (q, _) in enumerate(part))
            ds = sum(d * 8**k for k, (_, d) in enumerate(part))

            def step(k, carry):
                qs, ds = carry
                body(qs % 8, ds % 8)
                return qs // 8, ds // 8

            lax.fori_loop(0, len(part), step, (jnp.int32(qs), jnp.int32(ds)))

    def block(q):
        return (y + q // 2) % NY, (xh + q % 2) % NX

    def full(yc, xc, d):
        return ((yc // 2) * NX + xc) * ND + d

    def d_copy(s):
        return remote(dsend.at[s], drecv.at[s], d_ssem.at[s], d_rsem.at[s], other_core)

    def x_copy(d, xc):
        e = xc * ND + d
        to = ((1 - lo) * 2 + core, at(y, jnp.where(d == 0, 1 - xh, xh), z))
        return remote(xsend.at[e], xrecv.at[e], x_ssem.at[e], x_rsem.at[e], to)

    def away(yc, d):
        return jnp.where((yc + y) % 2 == 0, d, (NZ - d) % NZ)

    def a_copy(d, xc):
        e = xc * ND + d
        return remote(
            direct.at[e], columns(xc, z), a_ssem.at[e], a_rsem.at[e],
            z_off(away(rank, d)),
        )

    def a_local(xc):
        e = xc * ND
        return pltpu.make_async_copy(direct.at[e], columns(xc, z), a_rsem.at[e])

    def b_place(d, x_):
        return columns(x_, (z + away(rank, d)) % NZ)

    def b_copy(d, xc):
        e, r = xc * ND + d, xh * ND + d
        return remote(
            flipped.at[e], b_place(d, xh), b_ssem.at[e], b_rsem.at[r], mirror(xc)
        )

    def b_local(d, x_):
        e = x_ * ND + d
        return pltpu.make_async_copy(flipped.at[e], b_place(d, x_), b_rsem.at[e])

    def along_z(q):
        return jnp.logical_or(q == 5, q == 1)

    def goes_direct(q, d):
        return jnp.logical_or(d < ND - 1, along_z(q))

    def goes_flipped(q, d):
        last = jnp.logical_and(d == ND - 1, along_z(q))
        return jnp.logical_and(d > 0, jnp.logical_not(last))

    def left(yc, d):
        side = jnp.where(yc // 2 == lo, xh, 1 - xh)
        return rows[jnp.where(d == 0, y * NX + side, NQ + away(yc, d) - 1)]

    def place(t, yc, xc, d):
        s = full(yc, xc, d)

        @pl.when(yc % 2 != core)
        def _():
            dsend[s] = t.astype(BF16)
            d_copy(s).start()

        @pl.when(yc % 2 == core)
        def _():
            acc[s] = t

    def product(a, b):
        return lax.dot_general(
            a, b, (((1,), (1,)), ((), ())), preferred_element_type=F32
        )

    def multiply(q, d):
        yc, xc = block(q)
        place(product(left(yc, d), rows[yc * NX + xc]), yc, xc, d)

    def multiply_both(yc, d):
        n, depth = src.shape
        b = rows[pl.ds(yc * NX, NX)].reshape(NX * n, depth)
        t = product(left(yc, d), b)
        for xc in range(NX):
            place(t[:, xc * n : (xc + 1) * n], yc, xc, d)

    def pairs(todo):
        each(todo, lambda q, d: multiply_both((y + q // 2) % NY, d))

    def all_pairs(d):
        def step(k, carry):
            multiply_both(((k // 2 + 1 + lo) % 2) * 2 + k % 2, d)
            return carry

        lax.fori_loop(0, NY, step, 0)

    def pass_on(q, d):
        yc, xc = block(q)
        s, e = full(yc, xc, d), xc * ND + d

        @pl.when(jnp.logical_and(yc % 2 == core, yc // 2 != lo))
        def _():
            d_copy(s).wait_recv()
            xsend[e] = (acc[s] + drecv[s].astype(F32)).astype(BF16)
            x_copy(d, xc).start()

    def finish(q, d):
        yc, xc = block(q)
        s, e = full(yc, xc, d), xc * ND + d

        @pl.when(yc == rank)
        def _():
            d_copy(s).wait_recv()
            x_copy(d, xc).wait_recv()
            v = acc[s] + drecv[s].astype(F32) + xrecv[e].astype(F32)

            @pl.when(goes_direct(q, d))
            def _():
                direct[e] = v.astype(BF16)

                @pl.when(d == 0)
                def _():
                    a_local(xc).start()

                @pl.when(d > 0)
                def _():
                    a_copy(d, xc).start()

            @pl.when(goes_flipped(q, d))
            def _():
                flipped[e] = v.T.astype(BF16)

                @pl.when(q == 0)
                def _():
                    b_local(d, xh).start()

                @pl.when(q > 0)
                def _():
                    b_copy(d, xc).start()

    down[0].wait_recv()
    down[1].start()
    up[0].wait_recv()
    up[1].start()
    q_wait(0, 1)
    q_sends[5].start()
    q_wait(1, 0)
    q_sends[3].start()
    q_sends[4].start()
    pairs(((0, 1), (0, 0)))
    q_wait(3, 0)
    each(((2, 1), (6, 1)), multiply)
    each(FIRST, pass_on)

    down[1].wait_recv()
    down[2].start()
    up[1].wait_recv()
    up[2].start()
    q_wait(3, 1)
    q_sends[7].start()
    q_wait(1, 1)
    q_sends[6].start()
    pairs(((2, 2), (6, 2), (0, 2)))
    each(SECOND[:6], pass_on)
    q_wait(2, 0)
    each(SECOND[6:10], multiply)
    each(SECOND[6:10], pass_on)
    pairs(((6, 0),))
    each(SECOND[10:], pass_on)
    each(FIRST, finish)
    q_wait_part(2, 1, 0)
    q_wait_part(2, 1, 1)
    each(LATE, multiply)
    each(LATE, pass_on)
    pairs(((2, 0), (4, 0)))
    each(KEPT, pass_on)

    down[2].wait_recv()
    down[3].start()
    up[2].wait_recv()
    up[3].start()
    all_pairs(3)
    each(THIRD, pass_on)
    each(SECOND, finish)
    each(THIRD, finish)
    each(LATE, finish)
    each(KEPT, finish)

    down[3].wait_recv()
    up[3].wait_recv()
    all_pairs(4)
    each(LAST, pass_on)
    each(LAST, finish)

    for c in down + up + q_sends:
        c.wait_send()

    def drain(q, d):
        yc, xc = block(q)

        @pl.when(yc % 2 != core)
        def _():
            d_copy(full(yc, xc, d)).wait_send()

        @pl.when(jnp.logical_and(yc % 2 == core, yc // 2 != lo))
        def _():
            x_copy(d, xc).wait_send()

        @pl.when(yc == rank)
        def _():
            @pl.when(goes_direct(q, d))
            def _():
                @pl.when(d == 0)
                def _():
                    a_local(xc).wait()

                @pl.when(d > 0)
                def _():
                    a_copy(d, xc).wait()

            @pl.when(jnp.logical_and(q > 0, goes_flipped(q, d)))
            def _():
                b_copy(d, xc).wait_send()

        @pl.when(jnp.logical_and((rank + q // 2) % NY == y, goes_flipped(q, d)))
        def _():
            b_local(d, (xh + q) % NX).wait()

    for units in STEPS:
        each(units, drain)


def solution(mesh):
    def local(factors):
        _, rows, depth = factors.shape
        tile = (rows, rows)
        n = NX * ND
        dma = pltpu.SemaphoreType.DMA
        blocks = pl.pallas_call(
            kernel,
            out_shape=jax.ShapeDtypeStruct((rows, NX * NZ * rows), BF16),
            in_specs=[pl.BlockSpec(memory_space=pltpu.HBM)],
            out_specs=pl.BlockSpec(memory_space=pl.ANY),
            scratch_shapes=[
                pltpu.VMEM((NQ + NZ - 1, rows, depth), BF16),
                pltpu.VMEM((2 * n, *tile), BF16),
                pltpu.VMEM((2 * n, *tile), BF16),
                pltpu.VMEM((2 * n, *tile), F32),
                pltpu.VMEM((n, *tile), BF16),
                pltpu.VMEM((n, *tile), BF16),
                pltpu.VMEM((n, *tile), BF16),
                pltpu.VMEM((n, *tile), BF16),
                dma((1,)),
                dma((NZ,)), dma((NZ,)),
                dma((8,)), dma((NQ + 2,)),
                dma((2 * n,)), dma((2 * n,)),
                dma((n,)), dma((n,)),
                dma((n,)), dma((n,)),
                dma((n,)), dma((n,)),
            ],
            compiler_params=pltpu.CompilerParams(
                collective_id=0, has_side_effects=True, vmem_limit_bytes=44 * 2**20
            ),
        )(factors[0])
        return blocks.astype(F32)

    return jax.shard_map(
        local,
        mesh=mesh,
        in_specs=(P("rank", "basis", None),),
        out_specs=P("basis", "rank"),
        check_vma=False,
    )
```

```python
import functools

import jax
import jax.numpy as jnp
from jax import lax
from jax.experimental import pallas as pl
from jax.experimental.pallas import tpu as pltpu
from jax.sharding import PartitionSpec as P

MESH = pl.DeviceIdType.MESH
NY, NX, NZ = 4, 2, 8
F32, BF16 = jnp.float32, jnp.bfloat16

NQ, ND = NY * NX, 5

def both(*pairs):
    return tuple((q, d) for p, d in pairs for q in (p, p + 1))


FIRST = both((0, 1), (0, 0)) + ((2, 1), (6, 1))
SECOND = both((2, 2), (6, 2), (0, 2)) + ((3, 1), (7, 1), (4, 2), (4, 1)) + both((6, 0))
LATE = ((5, 2), (5, 1))
THIRD = both((0, 3), (2, 3), (4, 3), (6, 3))
KEPT = both((2, 0), (4, 0))
LAST = both((0, 4), (2, 4), (4, 4), (6, 4))
STEPS = (FIRST, SECOND, LATE, THIRD, KEPT, LAST)


def kernel(
    src, out, rows, dsend, drecv, acc, xsend, xrecv, direct, flipped,
    own_sem, p_ssem, p_rsem, q_ssem, q_rsem, d_ssem, d_rsem, x_ssem, x_rsem,
    a_ssem, a_rsem, b_ssem, b_rsem,
):
    rank = lax.axis_index("rank")
    basis = lax.axis_index("basis")
    lo, core = rank // 2, rank % 2
    z = basis % NZ
    xh = (basis // NZ) % NX
    y = basis // (NZ * NX)

    def at(y_, x_, z_):
        return (y_ * NX + x_) * NZ + z_

    other_core = (lo * 2 + (1 - core), basis)
    other_lo = ((1 - lo) * 2 + core, basis)
    other_x = (rank, at(y, 1 - xh, z))
    beside = ((1 - lo) * 2 + core, at(y, 1 - xh, z))
    y_up = (rank, at((y + 1) % NY, xh, z))
    y_down = (rank, at((y + 3) % NY, xh, z))

    def z_off(d):
        return (rank, at(y, xh, (z + d) % NZ))

    z_up, z_down = z_off(1), z_off(NZ - 1)

    half = src.shape[0] // 2

    def columns(x_, z_):
        width = src.shape[0]
        start = pl.multiple_of((x_ * NZ + z_) * width, width)
        return out.at[:, pl.ds(start, width)]

    def mirror(x_):
        return (y, at(rank, x_, z))

    barrier = pltpu.get_barrier_semaphore()
    partners = [other_core, other_lo, other_x, beside, y_up, y_down]
    partners += [z_off(d) for d in range(1, NZ)]
    for who in partners:
        pl.semaphore_signal(barrier, inc=1, device_id=who, device_id_type=MESH)

    @pl.when(rank != y)
    def _():
        for x_ in range(NX):
            pl.semaphore_signal(
                barrier, inc=1, device_id=mirror(x_), device_id_type=MESH
            )

    pl.semaphore_wait(barrier, len(partners) + jnp.where(rank != y, NX, 0))

    def remote(a, b, ssem, rsem, who):
        return pltpu.make_async_remote_copy(
            src_ref=a, dst_ref=b, send_sem=ssem, recv_sem=rsem,
            device_id=who, device_id_type=MESH,
        )

    def p_block(d):
        return src if d == 0 else rows.at[NQ + d - 1]

    def p_down(d):
        a, b = p_block(d), p_block(d + 1)
        if d == 3:
            a, b = a.at[pl.ds(0, half)], b.at[pl.ds(0, half)]
        return remote(a, b, p_ssem.at[d], p_rsem.at[d], z_down)

    def p_up(d):
        a, b = p_block((NZ - d) % NZ), p_block(NZ - d - 1)
        if d == 3:
            a, b = a.at[pl.ds(half, half)], b.at[pl.ds(half, half)]
        return remote(a, b, p_ssem.at[4 + d], p_rsem.at[4 + d], z_up)

    def q_slot(dy, flip):
        return ((y + dy) % NY) * NX + (xh + flip) % NX

    def q_copy(i, dy, flip, who, part=None):
        at_slot = rows.at[q_slot(dy, flip)]
        a = src if (dy, flip) == (0, 0) else at_slot
        sem = q_slot(dy, flip)
        if part is not None:
            a, at_slot = (r.at[pl.ds(part * half, half)] for r in (a, at_slot))
            sem = NQ + part
        return remote(a, at_slot, q_ssem.at[i], q_rsem.at[sem], who)

    def q_wait(dy, flip):
        slot = q_slot(dy, flip)
        remote(
            src, rows.at[slot], q_ssem.at[0], q_rsem.at[slot], other_x
        ).wait_recv()

    def q_wait_part(dy, flip, part):
        place = rows.at[q_slot(dy, flip), pl.ds(part * half, half)]
        remote(
            src.at[pl.ds(0, half)], place, q_ssem.at[0], q_rsem.at[NQ + part], other_x
        ).wait_recv()

    down = [p_down(d) for d in range(4)]
    up = [p_up(d) for d in range(4)]
    q_sends = [
        q_copy(0, 0, 0, y_down),
        q_copy(1, 0, 0, y_up),
        q_copy(2, 0, 0, other_x),
        q_copy(3, 1, 0, y_down),
        q_copy(4, 1, 0, other_x),
        q_copy(5, 0, 1, y_up),
        q_copy(6, 1, 1, y_down, 0),
        q_copy(7, 3, 1, y_up, 1),
    ]
    down[0].start()
    up[0].start()
    q_sends[0].start()
    q_sends[1].start()
    q_sends[2].start()
    own = pltpu.make_async_copy(src, rows.at[q_slot(0, 0)], own_sem.at[0])
    own.start()
    own.wait()

    def each(units, body):
        for first in range(0, len(units), 10):
            part = units[first : first + 10]
            qs = sum(q * 8**k for k, (q, _) in enumerate(part))
            ds = sum(d * 8**k for k, (_, d) in enumerate(part))

            def step(k, carry):
                qs, ds = carry
                body(qs % 8, ds % 8)
                return qs // 8, ds // 8

            lax.fori_loop(0, len(part), step, (jnp.int32(qs), jnp.int32(ds)))

    def block(q):
        return (y + q // 2) % NY, (xh + q % 2) % NX

    def full(yc, xc, d):
        return ((yc // 2) * NX + xc) * ND + d

    def d_copy(s):
        return remote(dsend.at[s], drecv.at[s], d_ssem.at[s], d_rsem.at[s], other_core)

    def x_copy(d, xc):
        e = xc * ND + d
        to = ((1 - lo) * 2 + core, at(y, jnp.where(d == 0, 1 - xh, xh), z))
        return remote(xsend.at[e], xrecv.at[e], x_ssem.at[e], x_rsem.at[e], to)

    def away(yc, d):
        return jnp.where((yc + y) % 2 == 0, d, (NZ - d) % NZ)

    def a_copy(d, xc):
        e = xc * ND + d
        return remote(
            direct.at[e], columns(xc, z), a_ssem.at[e], a_rsem.at[e],
            z_off(away(rank, d)),
        )

    def a_local(xc):
        e = xc * ND
        return pltpu.make_async_copy(direct.at[e], columns(xc, z), a_rsem.at[e])

    def b_place(d, x_):
        return columns(x_, (z + away(rank, d)) % NZ)

    def b_copy(d, xc):
        e, r = xc * ND + d, xh * ND + d
        return remote(
            flipped.at[e], b_place(d, xh), b_ssem.at[e], b_rsem.at[r], mirror(xc)
        )

    def b_local(d, x_):
        e = x_ * ND + d
        return pltpu.make_async_copy(flipped.at[e], b_place(d, x_), b_rsem.at[e])

    def along_z(q):
        return jnp.logical_or(q == 5, q == 1)

    def goes_direct(q, d):
        return jnp.logical_or(d < ND - 1, along_z(q))

    def goes_flipped(q, d):
        last = jnp.logical_and(d == ND - 1, along_z(q))
        return jnp.logical_and(d > 0, jnp.logical_not(last))

    def left(yc, d):
        side = jnp.where(yc // 2 == lo, xh, 1 - xh)
        return rows[jnp.where(d == 0, y * NX + side, NQ + away(yc, d) - 1)]

    def place(t, yc, xc, d):
        s = full(yc, xc, d)

        @pl.when(yc % 2 != core)
        def _():
            dsend[s] = t.astype(BF16)
            d_copy(s).start()

        @pl.when(yc % 2 == core)
        def _():
            acc[s] = t

    def product(a, b):
        return lax.dot_general(
            a, b, (((1,), (1,)), ((), ())), preferred_element_type=F32
        )

    def multiply(q, d):
        yc, xc = block(q)
        place(product(left(yc, d), rows[yc * NX + xc]), yc, xc, d)

    def multiply_both(yc, d):
        n, depth = src.shape
        b = rows[pl.ds(yc * NX, NX)].reshape(NX * n, depth)
        t = product(left(yc, d), b)
        for xc in range(NX):
            place(t[:, xc * n : (xc + 1) * n], yc, xc, d)

    def pairs(todo):
        each(todo, lambda q, d: multiply_both((y + q // 2) % NY, d))

    def all_pairs(d):
        def step(k, carry):
            multiply_both(((k // 2 + 1 + lo) % 2) * 2 + k % 2, d)
            return carry

        lax.fori_loop(0, NY, step, 0)

    def pass_on(q, d):
        yc, xc = block(q)
        s, e = full(yc, xc, d), xc * ND + d

        @pl.when(jnp.logical_and(yc % 2 == core, yc // 2 != lo))
        def _():
            d_copy(s).wait_recv()
            xsend[e] = (acc[s] + drecv[s].astype(F32)).astype(BF16)
            x_copy(d, xc).start()

    def finish(q, d):
        yc, xc = block(q)
        s, e = full(yc, xc, d), xc * ND + d

        @pl.when(yc == rank)
        def _():
            d_copy(s).wait_recv()
            x_copy(d, xc).wait_recv()
            v = acc[s] + drecv[s].astype(F32) + xrecv[e].astype(F32)

            @pl.when(goes_direct(q, d))
            def _():
                direct[e] = v.astype(BF16)

                @pl.when(d == 0)
                def _():
                    a_local(xc).start()

                @pl.when(d > 0)
                def _():
                    a_copy(d, xc).start()

            @pl.when(goes_flipped(q, d))
            def _():
                flipped[e] = v.T.astype(BF16)

                @pl.when(q == 0)
                def _():
                    b_local(d, xh).start()

                @pl.when(q > 0)
                def _():
                    b_copy(d, xc).start()

    def two(yc, d, body):
        def step(k, carry):
            body((yc - y + NY) % NY * 2 + k, d)
            return carry

        lax.fori_loop(0, NX, step, 0)

    away_rank = (1 - lo) * 2 + core

    down[0].wait_recv()
    down[1].start()
    up[0].wait_recv()
    up[1].start()
    q_wait(0, 1)
    q_sends[5].start()
    q_wait(1, 0)
    q_sends[3].start()
    q_sends[4].start()
    pairs(((0, 1), (0, 0)))
    q_wait(3, 0)
    each(((2, 1), (6, 1)), multiply)
    each(FIRST, pass_on)

    down[1].wait_recv()
    down[2].start()
    up[1].wait_recv()
    up[2].start()
    q_wait(3, 1)
    q_sends[7].start()
    q_wait(1, 1)
    q_sends[6].start()
    pairs(((2, 2), (6, 2), (0, 2)))
    each(SECOND[:6], pass_on)
    q_wait(2, 0)
    each(SECOND[6:10], multiply)
    each(SECOND[6:10], pass_on)
    pairs(((6, 0),))
    each(SECOND[10:], pass_on)
    each(FIRST, finish)
    q_wait_part(2, 1, 0)
    q_wait_part(2, 1, 1)
    each(LATE, multiply)
    each(LATE, pass_on)
    pairs(((2, 0), (4, 0)))
    each(KEPT, pass_on)

    down[2].wait_recv()
    down[3].start()
    up[2].wait_recv()
    up[3].start()
    all_pairs(3)
    two(away_rank, 3, pass_on)
    each(SECOND, finish)
    each(LATE, finish)
    each(KEPT, finish)
    two(rank, 3, finish)

    down[3].wait_recv()
    up[3].wait_recv()
    all_pairs(4)
    two(away_rank, 4, pass_on)
    two(rank, 4, finish)

    for c in down + up + q_sends:
        c.wait_send()

    def drain(q, d):
        yc, xc = block(q)

        @pl.when(yc % 2 != core)
        def _():
            d_copy(full(yc, xc, d)).wait_send()

        @pl.when(jnp.logical_and(yc % 2 == core, yc // 2 != lo))
        def _():
            x_copy(d, xc).wait_send()

        @pl.when(yc == rank)
        def _():
            @pl.when(goes_direct(q, d))
            def _():
                @pl.when(d == 0)
                def _():
                    a_local(xc).wait()

                @pl.when(d > 0)
                def _():
                    a_copy(d, xc).wait()

            @pl.when(jnp.logical_and(q > 0, goes_flipped(q, d)))
            def _():
                b_copy(d, xc).wait_send()

        @pl.when(jnp.logical_and((rank + q // 2) % NY == y, goes_flipped(q, d)))
        def _():
            b_local(d, (xh + q) % NX).wait()

    for units in STEPS:
        each(units, drain)


def solution(mesh):
    def local(factors):
        _, rows, depth = factors.shape
        tile = (rows, rows)
        n = NX * ND
        dma = pltpu.SemaphoreType.DMA
        blocks = pl.pallas_call(
            kernel,
            out_shape=jax.ShapeDtypeStruct((rows, NX * NZ * rows), BF16),
            in_specs=[pl.BlockSpec(memory_space=pltpu.HBM)],
            out_specs=pl.BlockSpec(memory_space=pl.ANY),
            scratch_shapes=[
                pltpu.VMEM((NQ + NZ - 1, rows, depth), BF16),
                pltpu.VMEM((2 * n, *tile), BF16),
                pltpu.VMEM((2 * n, *tile), BF16),
                pltpu.VMEM((2 * n, *tile), F32),
                pltpu.VMEM((n, *tile), BF16),
                pltpu.VMEM((n, *tile), BF16),
                pltpu.VMEM((n, *tile), BF16),
                pltpu.VMEM((n, *tile), BF16),
                dma((1,)),
                dma((NZ,)), dma((NZ,)),
                dma((8,)), dma((NQ + 2,)),
                dma((2 * n,)), dma((2 * n,)),
                dma((n,)), dma((n,)),
                dma((n,)), dma((n,)),
                dma((n,)), dma((n,)),
            ],
            compiler_params=pltpu.CompilerParams(
                collective_id=0, has_side_effects=True, vmem_limit_bytes=44 * 2**20
            ),
        )(factors[0])
        return blocks.astype(F32)

    return jax.shard_map(
        local,
        mesh=mesh,
        in_specs=(P("rank", "basis", None),),
        out_specs=P("basis", "rank"),
        check_vma=False,
    )
```

```python
import functools

import jax
import jax.numpy as jnp
from jax import lax
from jax.experimental import pallas as pl
from jax.experimental.pallas import tpu as pltpu
from jax.sharding import PartitionSpec as P

MESH = pl.DeviceIdType.MESH
NY, NX, NZ = 4, 2, 8
F32, BF16 = jnp.float32, jnp.bfloat16

NQ, ND = NY * NX, 5

def both(*pairs):
    return tuple((q, d) for p, d in pairs for q in (p, p + 1))


FIRST = both((0, 1), (0, 0)) + ((2, 1), (6, 1))
SECOND = both((2, 2), (6, 2), (0, 2)) + ((3, 1), (7, 1), (4, 2), (4, 1)) + both((6, 0))
LATE = ((5, 2), (5, 1))
THIRD = both((0, 3), (2, 3), (4, 3), (6, 3))
KEPT = both((2, 0), (4, 0))
LAST = both((0, 4), (2, 4), (4, 4), (6, 4))
STEPS = (FIRST, SECOND, LATE, THIRD, KEPT, LAST)


def kernel(
    src, out, rows, dsend, drecv, acc, xsend, xrecv, direct, flipped,
    own_sem, p_ssem, p_rsem, q_ssem, q_rsem, d_ssem, d_rsem, x_ssem, x_rsem,
    a_ssem, a_rsem, b_ssem, b_rsem,
):
    rank = lax.axis_index("rank")
    basis = lax.axis_index("basis")
    lo, core = rank // 2, rank % 2
    z = basis % NZ
    xh = (basis // NZ) % NX
    y = basis // (NZ * NX)

    def at(y_, x_, z_):
        return (y_ * NX + x_) * NZ + z_

    other_core = (lo * 2 + (1 - core), basis)
    other_lo = ((1 - lo) * 2 + core, basis)
    other_x = (rank, at(y, 1 - xh, z))
    beside = ((1 - lo) * 2 + core, at(y, 1 - xh, z))
    y_up = (rank, at((y + 1) % NY, xh, z))
    y_down = (rank, at((y + 3) % NY, xh, z))

    def z_off(d):
        return (rank, at(y, xh, (z + d) % NZ))

    z_up, z_down = z_off(1), z_off(NZ - 1)

    half = src.shape[0] // 2

    def columns(x_, z_):
        width = src.shape[0]
        start = pl.multiple_of((x_ * NZ + z_) * width, width)
        return out.at[:, pl.ds(start, width)]

    def mirror(x_):
        return (y, at(rank, x_, z))

    barrier = pltpu.get_barrier_semaphore()
    partners = [other_core, other_lo, other_x, beside, y_up, y_down]
    partners += [z_off(d) for d in range(1, NZ)]
    for who in partners:
        pl.semaphore_signal(barrier, inc=1, device_id=who, device_id_type=MESH)

    @pl.when(rank != y)
    def _():
        for x_ in range(NX):
            pl.semaphore_signal(
                barrier, inc=1, device_id=mirror(x_), device_id_type=MESH
            )

    pl.semaphore_wait(barrier, len(partners) + jnp.where(rank != y, NX, 0))

    def remote(a, b, ssem, rsem, who):
        return pltpu.make_async_remote_copy(
            src_ref=a, dst_ref=b, send_sem=ssem, recv_sem=rsem,
            device_id=who, device_id_type=MESH,
        )

    def p_block(d):
        return src if d == 0 else rows.at[NQ + d - 1]

    def p_down(d):
        a, b = p_block(d), p_block(d + 1)
        if d == 3:
            a, b = a.at[pl.ds(0, half)], b.at[pl.ds(0, half)]
        return remote(a, b, p_ssem.at[d], p_rsem.at[d], z_down)

    def p_up(d):
        a, b = p_block((NZ - d) % NZ), p_block(NZ - d - 1)
        if d == 3:
            a, b = a.at[pl.ds(half, half)], b.at[pl.ds(half, half)]
        return remote(a, b, p_ssem.at[4 + d], p_rsem.at[4 + d], z_up)

    def q_slot(dy, flip):
        return ((y + dy) % NY) * NX + (xh + flip) % NX

    def q_copy(i, dy, flip, who, part=None):
        at_slot = rows.at[q_slot(dy, flip)]
        a = src if (dy, flip) == (0, 0) else at_slot
        sem = q_slot(dy, flip)
        if part is not None:
            a, at_slot = (r.at[pl.ds(part * half, half)] for r in (a, at_slot))
            sem = NQ + part
        return remote(a, at_slot, q_ssem.at[i], q_rsem.at[sem], who)

    def q_wait(dy, flip):
        slot = q_slot(dy, flip)
        remote(
            src, rows.at[slot], q_ssem.at[0], q_rsem.at[slot], other_x
        ).wait_recv()

    def q_wait_part(dy, flip, part):
        place = rows.at[q_slot(dy, flip), pl.ds(part * half, half)]
        remote(
            src.at[pl.ds(0, half)], place, q_ssem.at[0], q_rsem.at[NQ + part], other_x
        ).wait_recv()

    down = [p_down(d) for d in range(4)]
    up = [p_up(d) for d in range(4)]
    q_sends = [
        q_copy(0, 0, 0, y_down),
        q_copy(1, 0, 0, y_up),
        q_copy(2, 0, 0, other_x),
        q_copy(3, 1, 0, y_down),
        q_copy(4, 1, 0, other_x),
        q_copy(5, 0, 1, y_up),
        q_copy(6, 1, 1, y_down, 0),
        q_copy(7, 3, 1, y_up, 1),
    ]
    down[0].start()
    up[0].start()
    q_sends[0].start()
    q_sends[1].start()
    q_sends[2].start()
    own = pltpu.make_async_copy(src, rows.at[q_slot(0, 0)], own_sem.at[0])
    own.start()
    own.wait()

    def each(units, body):
        for first in range(0, len(units), 10):
            part = units[first : first + 10]
            qs = sum(q * 8**k for k, (q, _) in enumerate(part))
            ds = sum(d * 8**k for k, (_, d) in enumerate(part))

            def step(k, carry):
                qs, ds = carry
                body(qs % 8, ds % 8)
                return qs // 8, ds // 8

            lax.fori_loop(0, len(part), step, (jnp.int32(qs), jnp.int32(ds)))

    def block(q):
        return (y + q // 2) % NY, (xh + q % 2) % NX

    def full(yc, xc, d):
        return ((yc // 2) * NX + xc) * ND + d

    def d_copy(s):
        return remote(dsend.at[s], drecv.at[s], d_ssem.at[s], d_rsem.at[s], other_core)

    def x_copy(d, xc):
        e = xc * ND + d
        to = ((1 - lo) * 2 + core, at(y, jnp.where(d == 0, 1 - xh, xh), z))
        return remote(xsend.at[e], xrecv.at[e], x_ssem.at[e], x_rsem.at[e], to)

    def away(yc, d):
        return jnp.where((yc + y) % 2 == 0, d, (NZ - d) % NZ)

    def a_copy(d, xc):
        e = xc * ND + d
        return remote(
            direct.at[e], columns(xc, z), a_ssem.at[e], a_rsem.at[e],
            z_off(away(rank, d)),
        )

    def a_local(xc):
        e = xc * ND
        return pltpu.make_async_copy(direct.at[e], columns(xc, z), a_rsem.at[e])

    def b_place(d, x_):
        return columns(x_, (z + away(rank, d)) % NZ)

    def b_copy(d, xc):
        e, r = xc * ND + d, xh * ND + d
        return remote(
            flipped.at[e], b_place(d, xh), b_ssem.at[e], b_rsem.at[r], mirror(xc)
        )

    def b_local(d, x_):
        e = x_ * ND + d
        return pltpu.make_async_copy(flipped.at[e], b_place(d, x_), b_rsem.at[e])

    def along_z(q):
        return jnp.logical_or(q == 5, q == 1)

    def goes_direct(q, d):
        return jnp.logical_or(d < ND - 1, along_z(q))

    def goes_flipped(q, d):
        last = jnp.logical_and(d == ND - 1, along_z(q))
        return jnp.logical_and(d > 0, jnp.logical_not(last))

    def left(yc, d):
        side = jnp.where(yc // 2 == lo, xh, 1 - xh)
        return rows[jnp.where(d == 0, y * NX + side, NQ + away(yc, d) - 1)]

    def place(t, yc, xc, d):
        s = full(yc, xc, d)

        @pl.when(yc % 2 != core)
        def _():
            dsend[s] = t.astype(BF16)
            d_copy(s).start()

        @pl.when(yc % 2 == core)
        def _():
            acc[s] = t

    def product(a, b):
        return lax.dot_general(
            a, b, (((1,), (1,)), ((), ())), preferred_element_type=F32
        )

    def multiply(q, d):
        yc, xc = block(q)
        place(product(left(yc, d), rows[yc * NX + xc]), yc, xc, d)

    def multiply_both(yc, d):
        n, depth = src.shape
        b = rows[pl.ds(yc * NX, NX)].reshape(NX * n, depth)
        t = product(left(yc, d), b)
        for xc in range(NX):
            place(t[:, xc * n : (xc + 1) * n], yc, xc, d)

    def pairs(todo):
        each(todo, lambda q, d: multiply_both((y + q // 2) % NY, d))

    def all_pairs(d, first, last):
        def step(k, carry):
            multiply_both(((k // 2 + 1 + lo) % 2) * 2 + k % 2, d)
            return carry

        lax.fori_loop(first, last, step, 0)

    def pass_on(q, d):
        yc, xc = block(q)
        s, e = full(yc, xc, d), xc * ND + d

        @pl.when(jnp.logical_and(yc % 2 == core, yc // 2 != lo))
        def _():
            d_copy(s).wait_recv()
            xsend[e] = (acc[s] + drecv[s].astype(F32)).astype(BF16)
            x_copy(d, xc).start()

    def finish(q, d):
        yc, xc = block(q)
        s, e = full(yc, xc, d), xc * ND + d

        @pl.when(yc == rank)
        def _():
            d_copy(s).wait_recv()
            x_copy(d, xc).wait_recv()
            v = acc[s] + drecv[s].astype(F32) + xrecv[e].astype(F32)

            @pl.when(goes_direct(q, d))
            def _():
                direct[e] = v.astype(BF16)

                @pl.when(d == 0)
                def _():
                    a_local(xc).start()

                @pl.when(d > 0)
                def _():
                    a_copy(d, xc).start()

            @pl.when(goes_flipped(q, d))
            def _():
                flipped[e] = v.T.astype(BF16)

                @pl.when(q == 0)
                def _():
                    b_local(d, xh).start()

                @pl.when(q > 0)
                def _():
                    b_copy(d, xc).start()

    def two(yc, d, body):
        def step(k, carry):
            body((yc - y + NY) % NY * 2 + k, d)
            return carry

        lax.fori_loop(0, NX, step, 0)

    away_rank = (1 - lo) * 2 + core

    down[0].wait_recv()
    down[1].start()
    up[0].wait_recv()
    up[1].start()
    q_wait(0, 1)
    q_sends[5].start()
    q_wait(1, 0)
    q_sends[3].start()
    q_sends[4].start()
    pairs(((0, 1), (0, 0)))
    q_wait(3, 0)
    each(((2, 1), (6, 1)), multiply)
    each(FIRST, pass_on)

    down[1].wait_recv()
    down[2].start()
    up[1].wait_recv()
    up[2].start()
    q_wait(3, 1)
    q_sends[7].start()
    q_wait(1, 1)
    q_sends[6].start()
    pairs(((2, 2), (6, 2), (0, 2)))
    each(SECOND[:6], pass_on)
    q_wait(2, 0)
    each(SECOND[6:10], multiply)
    each(SECOND[6:10], pass_on)
    pairs(((6, 0),))
    each(SECOND[10:], pass_on)
    each(FIRST, finish)
    q_wait_part(2, 1, 0)
    q_wait_part(2, 1, 1)
    each(LATE, multiply)
    each(LATE, pass_on)
    pairs(((2, 0), (4, 0)))
    each(KEPT, pass_on)

    down[2].wait_recv()
    down[3].start()
    up[2].wait_recv()
    up[3].start()
    all_pairs(3, 0, 3)
    two(away_rank, 3, pass_on)
    all_pairs(3, 3, NY)
    each(SECOND, finish)
    each(LATE, finish)
    each(KEPT, finish)
    two(rank, 3, finish)

    down[3].wait_recv()
    up[3].wait_recv()
    all_pairs(4, 0, 3)
    two(away_rank, 4, pass_on)
    all_pairs(4, 3, NY)
    two(rank, 4, finish)

    for c in down + up + q_sends:
        c.wait_send()

    def drain(q, d):
        yc, xc = block(q)

        @pl.when(yc % 2 != core)
        def _():
            d_copy(full(yc, xc, d)).wait_send()

        @pl.when(jnp.logical_and(yc % 2 == core, yc // 2 != lo))
        def _():
            x_copy(d, xc).wait_send()

        @pl.when(yc == rank)
        def _():
            @pl.when(goes_direct(q, d))
            def _():
                @pl.when(d == 0)
                def _():
                    a_local(xc).wait()

                @pl.when(d > 0)
                def _():
                    a_copy(d, xc).wait()

            @pl.when(jnp.logical_and(q > 0, goes_flipped(q, d)))
            def _():
                b_copy(d, xc).wait_send()

        @pl.when(jnp.logical_and((rank + q // 2) % NY == y, goes_flipped(q, d)))
        def _():
            b_local(d, (xh + q) % NX).wait()

    for units in STEPS:
        each(units, drain)


def solution(mesh):
    def local(factors):
        _, rows, depth = factors.shape
        tile = (rows, rows)
        n = NX * ND
        dma = pltpu.SemaphoreType.DMA
        blocks = pl.pallas_call(
            kernel,
            out_shape=jax.ShapeDtypeStruct((rows, NX * NZ * rows), BF16),
            in_specs=[pl.BlockSpec(memory_space=pltpu.HBM)],
            out_specs=pl.BlockSpec(memory_space=pl.ANY),
            scratch_shapes=[
                pltpu.VMEM((NQ + NZ - 1, rows, depth), BF16),
                pltpu.VMEM((2 * n, *tile), BF16),
                pltpu.VMEM((2 * n, *tile), BF16),
                pltpu.VMEM((2 * n, *tile), F32),
                pltpu.VMEM((n, *tile), BF16),
                pltpu.VMEM((n, *tile), BF16),
                pltpu.VMEM((n, *tile), BF16),
                pltpu.VMEM((n, *tile), BF16),
                dma((1,)),
                dma((NZ,)), dma((NZ,)),
                dma((8,)), dma((NQ + 2,)),
                dma((2 * n,)), dma((2 * n,)),
                dma((n,)), dma((n,)),
                dma((n,)), dma((n,)),
                dma((n,)), dma((n,)),
            ],
            compiler_params=pltpu.CompilerParams(
                collective_id=0, has_side_effects=True, vmem_limit_bytes=44 * 2**20
            ),
        )(factors[0])
        return blocks.astype(F32)

    return jax.shard_map(
        local,
        mesh=mesh,
        in_specs=(P("rank", "basis", None),),
        out_specs=P("basis", "rank"),
        check_vma=False,
    )
```
